32 devices in a mesh: space: 16 (over z, y, x), orb: 2 (over core).
Axes of the slice: x: 2, y: 2, z: 4, core: 2. Of those that a mesh axis runs over, the one named last changes fastest.
Arguments:
- coefficients: float32 [2, 16, 128, 512], P(None, 'space', None, 'orb'), may hold values from -6 to 6
- margin: float32 [16, 16, 128, 128], P('space'), may hold values from -0.125 to 0.125
- step_matrix: float32 [16, 16, 128, 128], P('space'), may hold values from -0.1875 to 0.1875
- neighbours: int32 [16, 16], P('space'), may hold values from 0 to 15, as said below
- pattern: int32 [16, 16], P('space'), may hold values 0 or 1
Outputs:
- propagated: float32 [2, 16, 128, 512], P(None, 'space', None, 'orb')
- projections: float32 [2, 512, 512], P(None, 'space', 'orb')
The draws below stay inside these ranges and needn't reach their ends.
Inputs may be any that keep to these rules, and one draw needn't show every extreme that they name: neighbours[i, 0] = i; every other entry is an atom block of a spatial domain at most 2 domains away from that of block i (domain = block index); the block of slot 1 lies 2 domains ahead of block i and the block of slot 2 lies 2 domains behind it, each clipped to the first and last domain.
All inputs are finite; a program needn't handle non-finite values. No bound on the sum of `pattern` on one device may be relied on, other than what follows from the above.
Results may differ from the reference program's by a relative error of at most 0.0001.
Values sent between devices are 32-bit elements; how exact they have to be, the bound alone decides.
A program may use at most 64 MiB of HBM per device.

```python
import jax
import jax.numpy as jnp
from jax import lax

BLOCK = 128
BLK_DEV = 1
NB = 16
REACH_DEV = 2
ORDER = 4
DOMAINS = 16
BLOCKS = 16
ORBS = 512
ROWS = 2048


def draw_neighbours(key, part):
    row_ids = jnp.arange(BLOCKS, dtype=jnp.int32)
    home_domain = row_ids // BLK_DEV
    key_offset, key_slot = jax.random.split(key)
    offsets = jax.random.randint(key_offset, (BLOCKS, NB), -REACH_DEV, REACH_DEV + 1, dtype=jnp.int32)
    column_ids = jnp.arange(NB, dtype=jnp.int32)[None, :]
    offsets = jnp.where(column_ids == 1, REACH_DEV, jnp.where(column_ids == 2, -REACH_DEV, offsets))
    target_domain = jnp.clip(home_domain[:, None] + offsets, 0, DOMAINS - 1)
    slot_ids = jax.random.randint(key_slot, (BLOCKS, NB), 0, BLK_DEV, dtype=jnp.int32)
    chosen = target_domain * BLK_DEV + slot_ids
    return jnp.where(column_ids == 0, row_ids[:, None], chosen).astype(jnp.int32)


def with_ends(values, stream_key, smallest, top_value):
    longest = values.shape.index(max(values.shape))
    spots = []
    for shift in (0, 1):
        where = [jax.random.randint(jax.random.fold_in(stream_key, axis), (), 0, length) for axis, length in enumerate(values.shape)]
        where[longest] = (where[longest] + shift) % values.shape[longest]
        spots.append(tuple(where))
    return values.at[spots[0]].set(smallest).at[spots[1]].set(top_value)


def shard_levels(own_key, dims, shards, smallest, top_value):
    def one(axis_at, parts):
        draws = jax.random.uniform(jax.random.fold_in(jax.random.fold_in(own_key, 6), axis_at), (parts,), jnp.float32, smallest / len(shards), top_value / len(shards))
        return jnp.repeat(jnp.exp(draws), dims[axis_at] // parts).reshape((-1,) + (1,) * (len(dims) - axis_at - 1))

    loudness = one(*shards[0])
    for cut in shards[1:]:
        loudness = loudness * one(*cut)
    return loudness


def scatter_about(own_key, shape, deviation, bound, shards=(), kind=jnp.bfloat16):
    drawn = jax.random.normal(own_key, shape, jnp.float32) * deviation
    if len(shards) > 0:
        drawn = shard_levels(own_key, shape, shards, -0.22, 0.18) * drawn
    return jnp.clip(drawn, min=-bound, max=bound).astype(kind)


def setup_inputs(seed: int = 0) -> dict:
    splits = jax.random.split(jax.random.key(seed), 6)
    coefficients = scatter_about(splits[0], (2, BLOCKS, BLOCK, ORBS), 1.0, 6.0, ((1, 16), (3, 2)), jnp.float32)
    margin = scatter_about(splits[1], (BLOCKS, NB, BLOCK, BLOCK), (BLOCK * NB) ** -0.5, 0.125, ((0, 16),), jnp.float32)
    step_matrix = scatter_about(splits[2], (BLOCKS, NB, BLOCK, BLOCK), (BLOCK * NB // 2) ** -0.5, 0.1875, ((0, 16),), jnp.float32)
    neighbours = draw_neighbours(jax.random.fold_in(splits[5], 71), 0)
    pattern = with_ends((jax.random.randint(splits[4], (BLOCKS, NB), 0, 4) < 3).astype(jnp.int32), jax.random.fold_in(splits[4], 1), 0, 1)
    return dict(coefficients=coefficients, margin=margin, step_matrix=step_matrix, neighbours=neighbours, pattern=pattern)


def apply_blocks(matrix, neighbours, state):
    groups = BLOCKS // BLK_DEV
    matrix_groups = matrix.reshape(groups, BLK_DEV, NB, BLOCK, BLOCK)
    index_groups = neighbours.reshape(groups, BLK_DEV, NB)

    def one_group(operands):
        block_mat, block_idx = operands
        picked = state[block_idx]
        return jnp.einsum("rkab,rkbc->rac", block_mat, picked, precision=lax.Precision.HIGHEST)

    result = lax.map(one_group, (matrix_groups, index_groups))
    return result.reshape(BLOCKS, BLOCK, 2 * ORBS)


def reference(coefficients, margin, step_matrix, neighbours, pattern):
    column_ids = jnp.arange(NB, dtype=jnp.int32)[None, :]
    weights = jnp.where(column_ids == 0, jnp.float32(1.0), pattern.astype(jnp.float32))
    margin_live = margin * weights[:, :, None, None]
    step_live = step_matrix * weights[:, :, None, None]
    state = jnp.concatenate([coefficients[0], coefficients[1]], axis=-1)
    moved = state + apply_blocks(margin_live, neighbours, state)
    total = moved
    term = moved
    for order_index in range(1, ORDER + 1):
        image = apply_blocks(step_live, neighbours, term)
        term = jnp.concatenate([image[..., ORBS:], -image[..., :ORBS]], axis=-1) / order_index
        total = total + term
    propagated = jnp.stack([total[..., :ORBS], total[..., ORBS:]])
    old_real = coefficients[0].reshape(ROWS, ORBS)
    old_imag = coefficients[1].reshape(ROWS, ORBS)
    new_real = propagated[0].reshape(ROWS, ORBS)
    new_imag = propagated[1].reshape(ROWS, ORBS)
    highest = lax.Precision.HIGHEST
    proj_real = jnp.einsum("ra,rb->ab", old_real, new_real, precision=highest) + jnp.einsum("ra,rb->ab", old_imag, new_imag, precision=highest)
    proj_imag = jnp.einsum("ra,rb->ab", old_real, new_imag, precision=highest) - jnp.einsum("ra,rb->ab", old_imag, new_real, precision=highest)
    projections = jnp.stack([proj_real, proj_imag]) / ROWS
    return propagated, projections
```

```python
import functools

import jax
import jax.numpy as jnp
from jax import lax
from jax.experimental import pallas as pl
from jax.experimental.pallas import tpu as pltpu
from jax.sharding import PartitionSpec as P

REACH = 2
WIN = 2 * REACH + 1
ORDER = 4
GROUP = 4
BLOCK = 128
LANES = 128
HALF = BLOCK // 2
MESH = pl.DeviceIdType.MESH


def halves():
    lane = lax.broadcasted_iota(jnp.int32, (1, LANES), 1)
    return lane < LANES // 2


def swap(value):
    return pltpu.roll(value, LANES // 2, 1)


def split(value):
    high = value.astype(jnp.bfloat16)
    low = (value - high.astype(jnp.float32)).astype(jnp.bfloat16)
    return high, low


def product(high, low, both):
    wide = jnp.dot(high, both, preferred_element_type=jnp.float32)
    narrow = jnp.dot(low, both[:, :LANES], preferred_element_type=jnp.float32)
    return wide[:, :LANES] + wide[:, LANES:] + narrow


def kernel(
    spaces, coef, margin, step, nbr, pat, prop, proj,
    old, win, rows, mat_hi, mat_lo, both, total, old_hi, old_lo, part, got, back,
    a2a_s, a2a_r, mat_s, mat_r, fwd_s, fwd_r, old_s, old_r, oldx_s, oldx_r,
    halo_s, halo_r, back_s, back_r, part_s, part_r,
):
    share = proj.shape[1]
    quads = spaces // GROUP
    s = lax.axis_index("space")
    o = lax.axis_index("orb")
    q = s // GROUP
    m = s % GROUP
    base = q * GROUP
    other = 1 - o
    left = halves()

    barrier = pltpu.get_barrier_semaphore()

    @pl.loop(1, spaces)
    def _(j):
        pl.semaphore_signal(barrier, inc=1, device_id=((s + j) % spaces, o), device_id_type=MESH)

    pl.semaphore_signal(barrier, inc=1, device_id=(s, other), device_id_type=MESH)

    for t in range(2):
        columns = slice(t * LANES, (t + 1) * LANES)
        real = coef[0, 0, :, columns]
        imag = coef[1, 0, :, columns]
        old[o, 2 * t, m] = jnp.where(left, real, swap(imag))
        old[o, 2 * t + 1, m] = jnp.where(left, swap(real), imag)

    def compact(which, source):
        sums = [None] * WIN
        for k in range(nbr.shape[1]):
            block = source[0, k, pl.ds(pl.multiple_of(o * HALF, HALF), HALF), :]
            live = jnp.float32(1.0) if k == 0 else pat[0, k].astype(jnp.float32)
            for d in range(WIN):
                here = (nbr[0, k] == s + (d - REACH)).astype(jnp.float32) * live
                value = here * block
                sums[d] = value if sums[d] is None else sums[d] + value
        for d in range(WIN):
            rows[which, m, o, :, d * BLOCK:(d + 1) * BLOCK] = sums[d]

    compact(0, margin)

    for n in range(ORDER + 1):
        @pl.when(q == 0)
        def _():
            win[n, 0:REACH] = jnp.zeros((REACH, BLOCK, LANES), jnp.float32)

        @pl.when(q == quads - 1)
        def _():
            win[n, REACH + GROUP:] = jnp.zeros((REACH, BLOCK, LANES), jnp.float32)

    pl.semaphore_wait(barrier, spaces)

    def remote(src, dst, send, recv, where):
        return pltpu.make_async_remote_copy(
            src_ref=src, dst_ref=dst, send_sem=send, recv_sem=recv, device_id=where, device_id_type=MESH
        )

    def peer(j):
        return (m + j) % GROUP

    def a2a(j):
        return remote(old.at[o, peer(j), m], old.at[o, peer(j), m], a2a_s.at[j], a2a_r.at[j], (base + peer(j), o))

    def mat_copy(which, j):
        return remote(
            rows.at[which, m, o], rows.at[which, m, o], mat_s.at[which, j], mat_r.at[which, j], (base + peer(j), o)
        )

    def mat_forward(which, j):
        block = (m + GROUP - j) % GROUP
        return remote(
            rows.at[which, block, o], rows.at[which, block, o], fwd_s.at[which, j], fwd_r.at[which, j], (s, other)
        )

    def old_copy(j, i):
        g = (m + j + i) % GROUP
        return remote(old.at[o, g, m], old.at[o, g, m], old_s.at[j, i], old_r.at[j, i], (base + peer(j), o))

    def old_cross():
        return remote(old.at[o], old.at[o], oldx_s, oldx_r, (s, other))

    def halo_up(n):
        src = old.at[o, m, GROUP - REACH:GROUP] if n == 0 else win.at[n, GROUP:GROUP + REACH]
        return remote(src, win.at[n, 0:REACH], halo_s.at[n, 0], halo_r.at[n, 0], (s + GROUP, o))

    def halo_down(n):
        src = old.at[o, m, 0:REACH] if n == 0 else win.at[n, REACH:2 * REACH]
        return remote(
            src, win.at[n, REACH + GROUP:2 * REACH + GROUP], halo_s.at[n, 1], halo_r.at[n, 1], (s - GROUP, o)
        )

    def send_halo(n):
        @pl.when(q < quads - 1)
        def _():
            halo_up(n).start()

        @pl.when(q > 0)
        def _():
            halo_down(n).start()

    def wait_halo(n):
        @pl.when(q > 0)
        def _():
            halo_up(n).wait_recv()

        @pl.when(q < quads - 1)
        def _():
            halo_down(n).wait_recv()

    def done_halo(n):
        @pl.when(q < quads - 1)
        def _():
            halo_up(n).wait_send()

        @pl.when(q > 0)
        def _():
            halo_down(n).wait_send()

    def put(block, value):
        high, low = split(value)
        both[block * BLOCK:(block + 1) * BLOCK, :LANES] = high
        both[block * BLOCK:(block + 1) * BLOCK, LANES:] = low

    for j in range(1, GROUP):
        a2a(j).start()
    for j in range(1, GROUP):
        mat_copy(0, j).start()
    mat_forward(0, 0).start()
    compact(1, step)
    for j in range(1, GROUP):
        mat_copy(1, j).start()
    mat_forward(1, 0).start()

    for j in range(1, GROUP):
        a2a(j).wait_recv()
    send_halo(0)
    for j in range(1, GROUP):
        for i in range(1, GROUP):
            old_copy(j, i).start()
    for b in range(GROUP):
        put(REACH + b, old[o, m, b])

    def receive_matrix(which):
        for j in range(1, GROUP):
            mat_copy(which, j).wait_recv()
            mat_forward(which, j).start()
        for j in range(GROUP):
            mat_forward(which, j).wait_recv()
        for b in range(GROUP):
            for h in range(2):
                high, low = split(rows[which, b, h])
                mat_hi[which, b, h * HALF:(h + 1) * HALF] = high
                mat_lo[which, b, h * HALF:(h + 1) * HALF] = low

    def piece(which, b, first, last):
        columns = slice((first - b) * BLOCK, (last - b) * BLOCK)
        return product(
            mat_hi[which, b, :, columns], mat_lo[which, b, :, columns], both[first * BLOCK:last * BLOCK]
        )

    def inner(which):
        return [
            piece(which, b, max(b, REACH), min(b + WIN, REACH + GROUP)) for b in range(GROUP)
        ]

    def outer(which, n, sums):
        wait_halo(n)
        for w in (*range(REACH), *range(REACH + GROUP, 2 * REACH + GROUP)):
            put(w, win[n, w])
        result = []
        for b in range(GROUP):
            value = sums[b]
            if b < REACH:
                value = value + piece(which, b, b, REACH)
            if b + WIN > REACH + GROUP:
                value = value + piece(which, b, REACH + GROUP, b + WIN)
            result.append(value)
        return result

    receive_matrix(0)
    image = outer(0, 0, inner(0))
    for b in range(GROUP):
        moved = old[o, m, b] + image[b]
        win[1, REACH + b] = moved
        total[b] = moved
    send_halo(1)
    for b in range(GROUP):
        put(REACH + b, win[1, REACH + b])
    receive_matrix(1)

    for n in range(1, ORDER + 1):
        sums = inner(1)
        if n == 2:
            for j in range(1, GROUP):
                for i in range(1, GROUP):
                    old_copy(j, i).wait_recv()
            old_cross().start()
        if n == ORDER:
            old_cross().wait_recv()
            for core in range(2):
                for g in range(GROUP):
                    flat = old[core, g].reshape(GROUP * BLOCK, LANES)
                    high, low = split(flat.T)
                    old_hi[core * GROUP + g] = high
                    old_lo[core * GROUP + g] = low
        image = outer(1, n, sums)
        scale = jnp.where(left, jnp.float32(1.0 / n), jnp.float32(-1.0 / n))
        terms = [swap(value) * scale for value in image]
        if n < ORDER:
            for b in range(GROUP):
                win[n + 1, REACH + b] = terms[b]
            send_halo(n + 1)
        for b in range(GROUP):
            value = total[b] + terms[b]
            total[b] = value
            put(REACH + b, terms[b] if n < ORDER else value)

    def back_copy(j):
        return remote(total.at[peer(j)], back.at[m], back_s.at[j], back_r.at[j], (base + peer(j), o))

    for j in range(1, GROUP):
        back_copy(j).start()
    back[m] = total[m]

    sign = jnp.where(left, jnp.float32(1.0), jnp.float32(-1.0))
    new = both[REACH * BLOCK:(REACH + GROUP) * BLOCK]
    per = HALF // share
    for g in range(2 * GROUP):
        value = product(old_hi[g], old_lo[g], new)
        value = value[:HALF] + swap(value[HALF:]) * sign
        for r in range(per):
            part[g * per + r] = value[r * share:(r + 1) * share]

    def part_copy(j):
        to = (s + j) % spaces
        return remote(part.at[to], got.at[s], part_s.at[j], part_r.at[j], (to, o))

    @pl.loop(1, spaces)
    def _(j):
        part_copy(j).start()

    got[s] = part[s]

    for j in range(1, GROUP):
        back_copy(j).wait_recv()
    for t in range(2):
        columns = slice(t * LANES, (t + 1) * LANES)
        first = back[2 * t]
        second = back[2 * t + 1]
        prop[0, 0, :, columns] = jnp.where(left, first, swap(second))
        prop[1, 0, :, columns] = jnp.where(left, swap(first), second)

    for j in range(1, GROUP):
        a2a(j).wait_send()
        for which in range(2):
            mat_copy(which, j).wait_send()
        for i in range(1, GROUP):
            old_copy(j, i).wait_send()
        back_copy(j).wait_send()
    for j in range(GROUP):
        for which in range(2):
            mat_forward(which, j).wait_send()
    old_cross().wait_send()
    for n in range(ORDER + 1):
        done_halo(n)

    @pl.loop(1, spaces)
    def _(j):
        part_copy(j).wait_recv()

    sums = []
    for g in range(GROUP):
        value = got[g]
        for r in range(1, quads):
            value = value + got[r * GROUP + g]
        sums.append(value * (1.0 / (spaces * BLOCK)))
    for t in range(2):
        columns = slice(t * LANES, (t + 1) * LANES)
        first, second = sums[2 * t], sums[2 * t + 1]
        proj[0, :, columns] = jnp.where(left, first, swap(second))
        proj[1, :, columns] = jnp.where(left, swap(first), second)

    @pl.loop(1, spaces)
    def _(j):
        part_copy(j).wait_send()


def solution(mesh):
    spaces = mesh.shape["space"]
    dma = pltpu.SemaphoreType.DMA
    f32, bf16 = jnp.float32, jnp.bfloat16

    def local(coefficients, margin, step_matrix, neighbours, pattern):
        share = 2 * coefficients.shape[3] // spaces
        vmem = pl.BlockSpec(memory_space=pltpu.VMEM)
        smem = pl.BlockSpec(memory_space=pltpu.SMEM)
        return pl.pallas_call(
            functools.partial(kernel, spaces),
            out_shape=(
                jax.ShapeDtypeStruct(coefficients.shape, f32),
                jax.ShapeDtypeStruct((2, share, coefficients.shape[3]), f32),
            ),
            in_specs=[vmem, vmem, vmem, smem, smem],
            out_specs=(vmem, vmem),
            scratch_shapes=[
                pltpu.VMEM((2, GROUP, GROUP, BLOCK, LANES), f32),
                pltpu.VMEM((ORDER + 1, 2 * REACH + GROUP, BLOCK, LANES), f32),
                pltpu.VMEM((2, GROUP, 2, HALF, WIN * BLOCK), f32),
                pltpu.VMEM((2, GROUP, BLOCK, WIN * BLOCK), bf16),
                pltpu.VMEM((2, GROUP, BLOCK, WIN * BLOCK), bf16),
                pltpu.VMEM(((2 * REACH + GROUP) * BLOCK, 2 * LANES), bf16),
                pltpu.VMEM((GROUP, BLOCK, LANES), f32),
                pltpu.VMEM((2 * GROUP, LANES, GROUP * BLOCK), bf16),
                pltpu.VMEM((2 * GROUP, LANES, GROUP * BLOCK), bf16),
                pltpu.VMEM((spaces, share, LANES), f32),
                pltpu.VMEM((spaces, share, LANES), f32),
                pltpu.VMEM((GROUP, BLOCK, LANES), f32),
                dma((GROUP,)), dma((GROUP,)),
                dma((2, GROUP)), dma((2, GROUP)),
                dma((2, GROUP)), dma((2, GROUP)),
                dma((GROUP, GROUP)), dma((GROUP, GROUP)),
                dma, dma,
                dma((ORDER + 1, 2)), dma((ORDER + 1, 2)),
                dma((GROUP,)), dma((GROUP,)),
                dma((spaces,)), dma((spaces,)),
            ],
            compiler_params=pltpu.CompilerParams(
                collective_id=0, has_side_effects=True, vmem_limit_bytes=40 * 1024 * 1024
            ),
            cost_estimate=pl.CostEstimate(flops=1200000000, bytes_accessed=3000000, transcendentals=0),
        )(coefficients, margin, step_matrix, neighbours, pattern)

    return jax.shard_map(
        local,
        mesh=mesh,
        in_specs=(
            P(None, "space", None, "orb"),
            P("space", None, None, None),
            P("space", None, None, None),
            P("space", None),
            P("space", None),
        ),
        out_specs=(P(None, "space", None, "orb"), P(None, "space", "orb")),
        check_vma=False,
    )
```

```python
import functools

import jax
import jax.numpy as jnp
from jax import lax
from jax.experimental import pallas as pl
from jax.experimental.pallas import tpu as pltpu
from jax.sharding import PartitionSpec as P

REACH = 2
WIN = 2 * REACH + 1
ORDER = 4
GROUP = 4
BLOCK = 128
LANES = 128
HALF = BLOCK // 2
MESH = pl.DeviceIdType.MESH


def halves():
    lane = lax.broadcasted_iota(jnp.int32, (1, LANES), 1)
    return lane < LANES // 2


def swap(value):
    return pltpu.roll(value, LANES // 2, 1)


def split(value):
    high = value.astype(jnp.bfloat16)
    low = (value - high.astype(jnp.float32)).astype(jnp.bfloat16)
    return high, low


def product(high, low, both):
    wide = jnp.dot(high, both, preferred_element_type=jnp.float32)
    narrow = jnp.dot(low, both[:, :LANES], preferred_element_type=jnp.float32)
    return wide[:, :LANES] + wide[:, LANES:] + narrow


def kernel(
    spaces, coef_in, margin_in, step_in, nbr_in, pat_in, prop, proj,
    coef, raw, nbr, pat, load_sem, old, win, rows, mat_hi, mat_lo, both, total, old_hi, old_lo, part, got, back,
    a2a_s, a2a_r, mat_s, mat_r, dia_s, dia_r, fwd_s, fwd_r, old_s, old_r, oldx_s, oldx_r,
    halo_s, halo_r, back_s, back_r, part_s, part_r,
):
    share = proj.shape[1]
    quads = spaces // GROUP
    s = lax.axis_index("space")
    o = lax.axis_index("orb")
    q = s // GROUP
    m = s % GROUP
    base = q * GROUP
    other = 1 - o
    left = halves()
    beside = (m + 1 - 2 * (m % 2), (m + GROUP // 2) % GROUP)
    blocks = (m, beside[0], beside[1], (beside[0] + GROUP // 2) % GROUP)
    mine = pl.ds(pl.multiple_of(o * HALF, HALF), HALF)

    loads = [
        pltpu.make_async_copy(coef_in.at[:, 0], coef, load_sem.at[0]),
        pltpu.make_async_copy(nbr_in, nbr, load_sem.at[1]),
        pltpu.make_async_copy(pat_in, pat, load_sem.at[2]),
        pltpu.make_async_copy(margin_in.at[0, :, mine], raw.at[0], load_sem.at[3]),
        pltpu.make_async_copy(step_in.at[0, :, mine], raw.at[1], load_sem.at[4]),
    ]
    for load in loads:
        load.start()

    barrier = pltpu.get_barrier_semaphore()

    @pl.loop(1, spaces)
    def _(j):
        pl.semaphore_signal(barrier, inc=1, device_id=((s + j) % spaces, o), device_id_type=MESH)

    pl.semaphore_signal(barrier, inc=1, device_id=(s, other), device_id_type=MESH)

    loads[0].wait()
    for t in range(2):
        columns = slice(t * LANES, (t + 1) * LANES)
        real = coef[0, :, columns]
        imag = coef[1, :, columns]
        old[o, 2 * t, m] = jnp.where(left, real, swap(imag))
        old[o, 2 * t + 1, m] = jnp.where(left, swap(real), imag)

    def compact(which):
        sums = [None] * WIN
        for k in range(nbr.shape[1]):
            block = raw[which, k]
            live = jnp.float32(1.0) if k == 0 else pat[0, k].astype(jnp.float32)
            for d in range(WIN):
                here = (nbr[0, k] == s + (d - REACH)).astype(jnp.float32) * live
                value = here * block
                sums[d] = value if sums[d] is None else sums[d] + value
        for d in range(WIN):
            for p in range(2):
                rows[which, m, o, p, :, d * BLOCK:(d + 1) * BLOCK] = sums[d][p * HALF // 2:(p + 1) * HALF // 2]

    for n in range(ORDER + 1):
        @pl.when(q == 0)
        def _():
            win[n, 0:REACH] = jnp.zeros((REACH, BLOCK, LANES), jnp.float32)

        @pl.when(q == quads - 1)
        def _():
            win[n, REACH + GROUP:] = jnp.zeros((REACH, BLOCK, LANES), jnp.float32)

    pl.semaphore_wait(barrier, spaces)

    def remote(src, dst, send, recv, where):
        return pltpu.make_async_remote_copy(
            src_ref=src, dst_ref=dst, send_sem=send, recv_sem=recv, device_id=where, device_id_type=MESH
        )

    def peer(j):
        return (m + j) % GROUP

    def a2a(j):
        return remote(old.at[o, peer(j), m], old.at[o, peer(j), m], a2a_s.at[j], a2a_r.at[j], (base + peer(j), o))

    def mat_copy(which, axis, p):
        src = rows.at[which, m, o, p]
        return remote(src, src, mat_s.at[which, axis, p], mat_r.at[which, axis, p], (base + beside[axis], o))

    def mat_relay(which, p):
        src = rows.at[which, beside[p], o, p]
        return remote(src, src, dia_s.at[which, p], dia_r.at[which, p], (base + beside[1 - p], o))

    def mat_cross(which, i, p):
        src = rows.at[which, blocks[i], o, p]
        return remote(src, src, fwd_s.at[which, i, p], fwd_r.at[which, i, p], (s, other))

    def old_copy(j, i):
        g = (m + j + i) % GROUP
        return remote(old.at[o, g, m], old.at[o, g, m], old_s.at[j, i], old_r.at[j, i], (base + peer(j), o))

    def old_cross():
        return remote(old.at[o], old.at[o], oldx_s, oldx_r, (s, other))

    def halo_up(n):
        src = old.at[o, m, GROUP - REACH:GROUP] if n == 0 else win.at[n, GROUP:GROUP + REACH]
        return remote(src, win.at[n, 0:REACH], halo_s.at[n, 0], halo_r.at[n, 0], (s + GROUP, o))

    def halo_down(n):
        src = old.at[o, m, 0:REACH] if n == 0 else win.at[n, REACH:2 * REACH]
        return remote(
            src, win.at[n, REACH + GROUP:2 * REACH + GROUP], halo_s.at[n, 1], halo_r.at[n, 1], (s - GROUP, o)
        )

    def send_halo(n):
        @pl.when(q < quads - 1)
        def _():
            halo_up(n).start()

        @pl.when(q > 0)
        def _():
            halo_down(n).start()

    def wait_halo(n):
        @pl.when(q > 0)
        def _():
            halo_up(n).wait_recv()

        @pl.when(q < quads - 1)
        def _():
            halo_down(n).wait_recv()

    def done_halo(n):
        @pl.when(q < quads - 1)
        def _():
            halo_up(n).wait_send()

        @pl.when(q > 0)
        def _():
            halo_down(n).wait_send()

    def put(block, value):
        high, low = split(value)
        both[block * BLOCK:(block + 1) * BLOCK, :LANES] = high
        both[block * BLOCK:(block + 1) * BLOCK, LANES:] = low

    for j in range(1, GROUP):
        a2a(j).start()
    for load in loads[1:4]:
        load.wait()

    def send_matrix(which):
        for p in range(2):
            mat_copy(which, p, p).start()
        for p in range(2):
            mat_copy(which, 1 - p, p).start()
        for p in range(2):
            mat_cross(which, 0, p).start()

    def relay_matrix(which):
        for p in range(2):
            mat_copy(which, p, p).wait_recv()
            mat_relay(which, p).start()
            mat_cross(which, 1 + p, p).start()

    compact(0)
    send_matrix(0)
    loads[4].wait()
    compact(1)

    for j in range(1, GROUP):
        a2a(j).wait_recv()
    send_halo(0)
    for b in range(GROUP):
        put(REACH + b, old[o, m, b])
    relay_matrix(0)
    send_matrix(1)

    def receive_matrix(which):
        for p in range(2):
            mat_copy(which, 1 - p, p).wait_recv()
            mat_cross(which, 2 - p, p).start()
        for p in range(2):
            mat_relay(which, p).wait_recv()
            mat_cross(which, 3, p).start()
        for i in range(GROUP):
            for p in range(2):
                mat_cross(which, i, p).wait_recv()
        for b in range(GROUP):
            for h in range(2):
                high, low = split(rows[which, b, h].reshape(HALF, WIN * BLOCK))
                mat_hi[which, b, h * HALF:(h + 1) * HALF] = high
                mat_lo[which, b, h * HALF:(h + 1) * HALF] = low

    def piece(which, b, first, last):
        columns = slice((first - b) * BLOCK, (last - b) * BLOCK)
        return product(
            mat_hi[which, b, :, columns], mat_lo[which, b, :, columns], both[first * BLOCK:last * BLOCK]
        )

    def inner(which):
        return [
            piece(which, b, max(b, REACH), min(b + WIN, REACH + GROUP)) for b in range(GROUP)
        ]

    def outer(which, n, sums):
        wait_halo(n)
        for w in (*range(REACH), *range(REACH + GROUP, 2 * REACH + GROUP)):
            put(w, win[n, w])
        result = []
        for b in range(GROUP):
            value = sums[b]
            if b < REACH:
                value = value + piece(which, b, b, REACH)
            if b + WIN > REACH + GROUP:
                value = value + piece(which, b, REACH + GROUP, b + WIN)
            result.append(value)
        return result

    receive_matrix(0)
    image = outer(0, 0, inner(0))
    for b in range(GROUP):
        moved = old[o, m, b] + image[b]
        win[1, REACH + b] = moved
        total[b] = moved
    send_halo(1)
    for b in range(GROUP):
        put(REACH + b, win[1, REACH + b])
    relay_matrix(1)
    for j in range(1, GROUP):
        for i in range(1, GROUP):
            old_copy(j, i).start()
    receive_matrix(1)

    def turn(core):
        for g in range(GROUP):
            high, low = split(old[core, g].reshape(GROUP * BLOCK, LANES).T)
            old_hi[core * GROUP + g] = high
            old_lo[core * GROUP + g] = low

    for n in range(1, ORDER + 1):
        sums = inner(1)
        if n == ORDER - 1:
            for j in range(1, GROUP):
                for i in range(1, GROUP):
                    old_copy(j, i).wait_recv()
            old_cross().start()
            turn(o)
        if n == ORDER:
            old_cross().wait_recv()
            turn(other)
        image = outer(1, n, sums)
        scale = jnp.where(left, jnp.float32(1.0 / n), jnp.float32(-1.0 / n))
        terms = [swap(value) * scale for value in image]
        if n < ORDER:
            for b in range(GROUP):
                win[n + 1, REACH + b] = terms[b]
            send_halo(n + 1)
        for b in range(GROUP):
            value = total[b] + terms[b]
            total[b] = value
            put(REACH + b, terms[b] if n < ORDER else value)

    def back_copy(j):
        return remote(total.at[peer(j)], back.at[m], back_s.at[j], back_r.at[j], (base + peer(j), o))

    for j in range(1, GROUP):
        back_copy(j).start()
    back[m] = total[m]

    sign = jnp.where(left, jnp.float32(1.0), jnp.float32(-1.0))
    new = both[REACH * BLOCK:(REACH + GROUP) * BLOCK]
    per = HALF // share

    def part_copy(j):
        to = (s + j) % spaces
        return remote(part.at[to], got.at[s], part_s.at[j], part_r.at[j], (to, o))

    for i in range(2 * GROUP):
        g = (i + (q + quads // 2) * 2 * GROUP // quads) % (2 * GROUP)
        value = product(old_hi[g], old_lo[g], new)
        value = value[:HALF] + swap(value[HALF:]) * sign
        for r in range(per):
            to = g * per + r
            part[to] = value[r * share:(r + 1) * share]

            @pl.when(to != s)
            def _():
                part_copy((to - s + spaces) % spaces).start()

    got[s] = part[s]

    for j in range(1, GROUP):
        back_copy(j).wait_recv()
    for t in range(2):
        columns = slice(t * LANES, (t + 1) * LANES)
        first = back[2 * t]
        second = back[2 * t + 1]
        prop[0, 0, :, columns] = jnp.where(left, first, swap(second))
        prop[1, 0, :, columns] = jnp.where(left, swap(first), second)

    for j in range(1, GROUP):
        a2a(j).wait_send()
        for i in range(1, GROUP):
            old_copy(j, i).wait_send()
        back_copy(j).wait_send()
    for which in range(2):
        for p in range(2):
            mat_copy(which, 0, p).wait_send()
            mat_copy(which, 1, p).wait_send()
            mat_relay(which, p).wait_send()
            for i in range(GROUP):
                mat_cross(which, i, p).wait_send()
    old_cross().wait_send()
    for n in range(ORDER + 1):
        done_halo(n)

    @pl.loop(1, spaces)
    def _(j):
        part_copy(j).wait_recv()

    sums = []
    for g in range(GROUP):
        value = got[g]
        for r in range(1, quads):
            value = value + got[r * GROUP + g]
        sums.append(value * (1.0 / (spaces * BLOCK)))
    for t in range(2):
        columns = slice(t * LANES, (t + 1) * LANES)
        first, second = sums[2 * t], sums[2 * t + 1]
        proj[0, :, columns] = jnp.where(left, first, swap(second))
        proj[1, :, columns] = jnp.where(left, swap(first), second)

    @pl.loop(1, spaces)
    def _(j):
        part_copy(j).wait_send()


def solution(mesh):
    spaces = mesh.shape["space"]
    dma = pltpu.SemaphoreType.DMA
    f32, bf16 = jnp.float32, jnp.bfloat16

    def local(coefficients, margin, step_matrix, neighbours, pattern):
        share = 2 * coefficients.shape[3] // spaces
        vmem = pl.BlockSpec(memory_space=pltpu.VMEM)
        hbm = pl.BlockSpec(memory_space=pltpu.HBM)
        return pl.pallas_call(
            functools.partial(kernel, spaces),
            out_shape=(
                jax.ShapeDtypeStruct(coefficients.shape, f32),
                jax.ShapeDtypeStruct((2, share, coefficients.shape[3]), f32),
            ),
            in_specs=[hbm] * 5,
            out_specs=(vmem, vmem),
            scratch_shapes=[
                pltpu.VMEM((2,) + coefficients.shape[2:], f32),
                pltpu.VMEM((2, margin.shape[1], HALF, BLOCK), f32),
                pltpu.SMEM(neighbours.shape, jnp.int32),
                pltpu.SMEM(pattern.shape, jnp.int32),
                dma((5,)),
                pltpu.VMEM((2, GROUP, GROUP, BLOCK, LANES), f32),
                pltpu.VMEM((ORDER + 1, 2 * REACH + GROUP, BLOCK, LANES), f32),
                pltpu.VMEM((2, GROUP, 2, 2, HALF // 2, WIN * BLOCK), f32),
                pltpu.VMEM((2, GROUP, BLOCK, WIN * BLOCK), bf16),
                pltpu.VMEM((2, GROUP, BLOCK, WIN * BLOCK), bf16),
                pltpu.VMEM(((2 * REACH + GROUP) * BLOCK, 2 * LANES), bf16),
                pltpu.VMEM((GROUP, BLOCK, LANES), f32),
                pltpu.VMEM((2 * GROUP, LANES, GROUP * BLOCK), bf16),
                pltpu.VMEM((2 * GROUP, LANES, GROUP * BLOCK), bf16),
                pltpu.VMEM((spaces, share, LANES), f32),
                pltpu.VMEM((spaces, share, LANES), f32),
                pltpu.VMEM((GROUP, BLOCK, LANES), f32),
                dma((GROUP,)), dma((GROUP,)),
                dma((2, 2, 2)), dma((2, 2, 2)),
                dma((2, 2)), dma((2, 2)),
                dma((2, GROUP, 2)), dma((2, GROUP, 2)),
                dma((GROUP, GROUP)), dma((GROUP, GROUP)),
                dma, dma,
                dma((ORDER + 1, 2)), dma((ORDER + 1, 2)),
                dma((GROUP,)), dma((GROUP,)),
                dma((spaces,)), dma((spaces,)),
            ],
            compiler_params=pltpu.CompilerParams(
                collective_id=0, has_side_effects=True, vmem_limit_bytes=40 * 1024 * 1024
            ),
            cost_estimate=pl.CostEstimate(flops=1200000000, bytes_accessed=3000000, transcendentals=0),
        )(coefficients, margin, step_matrix, neighbours, pattern)

    return jax.shard_map(
        local,
        mesh=mesh,
        in_specs=(
            P(None, "space", None, "orb"),
            P("space", None, None, None),
            P("space", None, None, None),
            P("space", None),
            P("space", None),
        ),
        out_specs=(P(None, "space", None, "orb"), P(None, "space", "orb")),
        check_vma=False,
    )
```

```python
import functools

import jax
import jax.numpy as jnp
from jax import lax
from jax.experimental import pallas as pl
from jax.experimental.pallas import tpu as pltpu
from jax.sharding import PartitionSpec as P

REACH = 2
WIN = 2 * REACH + 1
ORDER = 4
GROUP = 4
BLOCK = 128
LANES = 128
HALF = BLOCK // 2
MESH = pl.DeviceIdType.MESH


CHUNKS = 2
QUARTER = LANES // 4


def lanes():
    return lax.broadcasted_iota(jnp.int32, (1, LANES), 1)


def pair(even, first, second):
    ahead = jnp.where(even, first, pltpu.roll(second, QUARTER, 1))
    behind = jnp.where(even, pltpu.roll(first, LANES - QUARTER, 1), second)
    return ahead, behind


def swap(even, value):
    return jnp.where(even, pltpu.roll(value, LANES - QUARTER, 1), pltpu.roll(value, QUARTER, 1))


def cross(left, first, second):
    ahead = jnp.where(left, first, pltpu.roll(second, LANES // 2, 1))
    behind = jnp.where(left, pltpu.roll(first, LANES // 2, 1), second)
    return ahead, behind


def split(value):
    high = value.astype(jnp.bfloat16)
    low = (value - high.astype(jnp.float32)).astype(jnp.bfloat16)
    return high, low


def product(high, low, both):
    wide = jnp.dot(high, both, preferred_element_type=jnp.float32)
    narrow = jnp.dot(low, both[:, :LANES], preferred_element_type=jnp.float32)
    return wide[:, :LANES] + wide[:, LANES:] + narrow


def kernel(
    spaces, coef_in, margin_in, step_in, nbr_in, pat_in, prop, proj,
    coef, raw, nbr, pat, load_sem, old, edge, halo, state, rows, mat, both, total, blocks_new, new, old_hi, old_lo, part, got, back,
    a2a_s, a2a_r, mat_s, mat_r, dia_s, dia_r, fwd_s, fwd_r, old_s, old_r, oldx_s, oldx_r,
    halo_s, halo_r, back_s, back_r, part_s, part_r,
):
    share = proj.shape[1]
    quads = spaces // GROUP
    s = lax.axis_index("space")
    o = lax.axis_index("orb")
    q = s // GROUP
    m = s % GROUP
    base = q * GROUP
    other = 1 - o
    left = lanes() < LANES // 2
    even = lanes() % (2 * QUARTER) < QUARTER
    beside = (m + 1 - 2 * (m % 2), (m + GROUP // 2) % GROUP)
    blocks = (m, beside[0], beside[1], (beside[0] + GROUP // 2) % GROUP)
    mine = pl.ds(pl.multiple_of(o * HALF, HALF), HALF)

    loads = [
        pltpu.make_async_copy(coef_in.at[:, 0], coef, load_sem.at[0]),
        pltpu.make_async_copy(nbr_in, nbr, load_sem.at[1]),
        pltpu.make_async_copy(pat_in, pat, load_sem.at[2]),
        pltpu.make_async_copy(margin_in.at[0, :, mine], raw.at[0], load_sem.at[3]),
        pltpu.make_async_copy(step_in.at[0, :, mine], raw.at[1], load_sem.at[4]),
    ]
    for load in loads:
        load.start()

    barrier = pltpu.get_barrier_semaphore()

    @pl.loop(1, spaces)
    def _(j):
        pl.semaphore_signal(barrier, inc=1, device_id=((s + j) % spaces, o), device_id_type=MESH)

    pl.semaphore_signal(barrier, inc=1, device_id=(s, other), device_id_type=MESH)

    loads[0].wait()
    for t in range(2):
        columns = slice(t * LANES, (t + 1) * LANES)
        real = coef[0, :, columns]
        imag = coef[1, :, columns]
        old[o, 2 * t, m], old[o, 2 * t + 1, m] = pair(even, real, imag)

    def compact(which):
        sums = [None] * WIN
        for k in range(nbr.shape[1]):
            block = raw[which, k]
            live = jnp.float32(1.0) if k == 0 else pat[0, k].astype(jnp.float32)
            for d in range(WIN):
                here = (nbr[0, k] == s + (d - REACH)).astype(jnp.float32) * live
                value = here * block
                sums[d] = value if sums[d] is None else sums[d] + value
        for d in range(WIN):
            for p in range(2):
                rows[which, m, o, p, :, d * BLOCK:(d + 1) * BLOCK] = sums[d][p * HALF // 2:(p + 1) * HALF // 2]

    def clear(side):
        zero = jnp.zeros((BLOCK, LANES), jnp.float32)
        for w in range(REACH):
            edge[side, w] = zero
        for n in range(ORDER):
            for c in range(CHUNKS):
                halo[n, c, side] = zero

    @pl.when(q == 0)
    def _():
        clear(0)

    @pl.when(q == quads - 1)
    def _():
        clear(1)

    pl.semaphore_wait(barrier, spaces)

    def remote(src, dst, send, recv, where):
        return pltpu.make_async_remote_copy(
            src_ref=src, dst_ref=dst, send_sem=send, recv_sem=recv, device_id=where, device_id_type=MESH
        )

    def peer(j):
        return (m + j) % GROUP

    def a2a(j):
        return remote(old.at[o, peer(j), m], old.at[o, peer(j), m], a2a_s.at[j], a2a_r.at[j], (base + peer(j), o))

    def mat_copy(which, axis, p):
        src = rows.at[which, m, o, p]
        return remote(src, src, mat_s.at[which, axis, p], mat_r.at[which, axis, p], (base + beside[axis], o))

    def mat_relay(which, p):
        src = rows.at[which, beside[p], o, p]
        return remote(src, src, dia_s.at[which, p], dia_r.at[which, p], (base + beside[1 - p], o))

    def mat_cross(which, i, p):
        src = rows.at[which, blocks[i], o, p]
        return remote(src, src, fwd_s.at[which, i, p], fwd_r.at[which, i, p], (s, other))

    def old_copy(j, i):
        g = (m + j + i) % GROUP
        return remote(old.at[o, g, m], old.at[o, g, m], old_s.at[j, i], old_r.at[j, i], (base + peer(j), o))

    def old_cross():
        return remote(old.at[o], old.at[o], oldx_s, oldx_r, (s, other))

    def halo_copy(n, c, up):
        side = 0 if up else 1
        if n == 0:
            src = old.at[o, m, REACH:GROUP] if up else old.at[o, m, 0:REACH]
            dst = edge.at[side]
        else:
            src, dst = state.at[n - 1, c, 1 - side], halo.at[n - 1, c, side]
        to = s + GROUP if up else s - GROUP
        return remote(src, dst, halo_s.at[n, c, side], halo_r.at[n, c, side], (to, o))

    def send_halo(n, c):
        @pl.when(q < quads - 1)
        def _():
            halo_copy(n, c, True).start()

        @pl.when(q > 0)
        def _():
            halo_copy(n, c, False).start()

    def wait_halo(n, c):
        @pl.when(q > 0)
        def _():
            halo_copy(n, c, True).wait_recv()

        @pl.when(q < quads - 1)
        def _():
            halo_copy(n, c, False).wait_recv()

    def done_halo(n, c):
        @pl.when(q < quads - 1)
        def _():
            halo_copy(n, c, True).wait_send()

        @pl.when(q > 0)
        def _():
            halo_copy(n, c, False).wait_send()

    def halves(value):
        high = value.astype(jnp.bfloat16).astype(jnp.float32)
        ahead, behind = cross(left, high, value - high)
        return ahead.astype(jnp.bfloat16), behind.astype(jnp.bfloat16)

    def span(w):
        return slice(w * BLOCK, (w + 1) * BLOCK)

    def put_block(w, value):
        both[0, span(w)], both[1, span(w)] = halves(value)

    def put_pair(c, w, value):
        both[c, span(w)], both[c, span(w + 1)] = halves(value)

    for j in range(1, GROUP):
        a2a(j).start()
    for load in loads[1:4]:
        load.wait()

    def send_matrix(which):
        for p in range(2):
            mat_copy(which, p, p).start()
        for p in range(2):
            mat_copy(which, 1 - p, p).start()
        for p in range(2):
            mat_cross(which, 0, p).start()

    def relay_matrix(which):
        for p in range(2):
            mat_copy(which, p, p).wait_recv()
            mat_relay(which, p).start()
            mat_cross(which, 1 + p, p).start()

    compact(0)
    send_matrix(0)
    loads[4].wait()
    compact(1)

    for j in range(1, GROUP):
        a2a(j).wait_recv()
    send_halo(0, 0)
    for b in range(GROUP):
        put_block(REACH + b, old[o, m, b])
    relay_matrix(0)
    send_matrix(1)

    def receive_matrix(which):
        for p in range(2):
            mat_copy(which, 1 - p, p).wait_recv()
            mat_cross(which, 2 - p, p).start()
        for p in range(2):
            mat_relay(which, p).wait_recv()
            mat_cross(which, 3, p).start()
        for i in range(GROUP):
            for p in range(2):
                mat_cross(which, i, p).wait_recv()
        for b in range(GROUP):
            for h in range(2):
                high, low = split(rows[which, b, h].reshape(HALF, WIN * BLOCK))
                mat[which, b, h * HALF:(h + 1) * HALF] = high
                mat[which, b, BLOCK + h * HALF:BLOCK + (h + 1) * HALF] = low

    def piece(which, c, b, first, last):
        columns = slice((first - b) * BLOCK, (last - b) * BLOCK)
        value = jnp.dot(
            mat[which, b, :, columns], both[c, first * BLOCK:last * BLOCK], preferred_element_type=jnp.float32
        )
        return value[:BLOCK] + value[BLOCK:]

    def inner(which, c):
        return [
            piece(which, c, b, max(b, REACH), min(b + WIN, REACH + GROUP)) for b in range(GROUP)
        ]

    def outer(which, c, sums):
        result = []
        for b in range(GROUP):
            value = sums[b]
            if b < REACH:
                value = value + piece(which, c, b, b, REACH)
            if b + WIN > REACH + GROUP:
                value = value + piece(which, c, b, REACH + GROUP, b + WIN)
            result.append(value + pltpu.roll(value, LANES // 2, 1))
        return [jnp.where(left, result[2 * i], result[2 * i + 1]) for i in range(GROUP // 2)]

    receive_matrix(0)
    sums = [inner(0, c) for c in range(CHUNKS)]
    wait_halo(0, 0)
    for side in range(2):
        for w in range(REACH):
            put_block(side * (REACH + GROUP) + w, edge[side, w])
    start = [cross(left, old[o, m, 2 * i], old[o, m, 2 * i + 1]) for i in range(GROUP // 2)]
    for c in range(CHUNKS):
        image = outer(0, c, sums[c])
        for i in range(GROUP // 2):
            moved = start[i][c] + image[i]
            state[0, c, i] = moved
            total[c, i] = moved
        send_halo(1, c)
    for c in range(CHUNKS):
        for i in range(GROUP // 2):
            put_pair(c, REACH + 2 * i, state[0, c, i])
    relay_matrix(1)
    for j in range(1, GROUP):
        for i in range(1, GROUP):
            old_copy(j, i).start()
    receive_matrix(1)

    def turn(core):
        for g in range(GROUP):
            high, low = split(old[core, g].reshape(GROUP * BLOCK, LANES).T)
            old_hi[core * GROUP + g] = high
            old_lo[core * GROUP + g] = low

    sums = [inner(1, c) for c in range(CHUNKS)]
    for n in range(1, ORDER + 1):
        if n == ORDER - 1:
            for j in range(1, GROUP):
                for i in range(1, GROUP):
                    old_copy(j, i).wait_recv()
            old_cross().start()
            turn(o)
        if n == ORDER:
            old_cross().wait_recv()
            turn(other)
        scale = jnp.where(even, jnp.float32(1.0 / n), jnp.float32(-1.0 / n))
        for c in range(CHUNKS):
            wait_halo(n, c)
            for side in range(2):
                put_pair(c, side * (REACH + GROUP), halo[n - 1, c, side])
            terms = [swap(even, value) * scale for value in outer(1, c, sums[c])]
            if n < ORDER:
                for i in range(GROUP // 2):
                    state[n, c, i] = terms[i]
                send_halo(n + 1, c)
            for i in range(GROUP // 2):
                total[c, i] = total[c, i] + terms[i]
            if n < ORDER:
                for i in range(GROUP // 2):
                    put_pair(c, REACH + 2 * i, terms[i])
                sums[c] = inner(1, c)

    for i in range(GROUP // 2):
        ends = cross(left, total[0, i], total[1, i])
        for h in range(2):
            blocks_new[2 * i + h] = ends[h]
            high, low = split(ends[h])
            new[span(2 * i + h), :LANES] = high
            new[span(2 * i + h), LANES:] = low

    def back_copy(j):
        return remote(blocks_new.at[peer(j)], back.at[m], back_s.at[j], back_r.at[j], (base + peer(j), o))

    for j in range(1, GROUP):
        back_copy(j).start()
    back[m] = blocks_new[m]

    sign = jnp.where(even, jnp.float32(1.0), jnp.float32(-1.0))
    per = QUARTER // share

    def part_copy(j):
        to = (s + j) % spaces
        return remote(part.at[to], got.at[s], part_s.at[j], part_r.at[j], (to, o))

    for i in range(2 * GROUP):
        g = (i + (q + quads // 2) * 2 * GROUP // quads) % (2 * GROUP)
        value = product(old_hi[g], old_lo[g], new[...])
        for c in range(CHUNKS):
            lead = 2 * c * QUARTER
            found = value[lead:lead + QUARTER] + swap(even, value[lead + QUARTER:lead + 2 * QUARTER]) * sign
            first = ((g // 2) * 4 + 2 * c + g % 2) * per
            for r in range(per):
                to = first + r
                part[to] = found[r * share:(r + 1) * share]

                @pl.when(to != s)
                def _():
                    part_copy((to - s + spaces) % spaces).start()

    got[s] = part[s]

    for j in range(1, GROUP):
        back_copy(j).wait_recv()
    for t in range(2):
        columns = slice(t * LANES, (t + 1) * LANES)
        prop[0, 0, :, columns], prop[1, 0, :, columns] = pair(even, back[2 * t], back[2 * t + 1])

    for j in range(1, GROUP):
        a2a(j).wait_send()
        for i in range(1, GROUP):
            old_copy(j, i).wait_send()
        back_copy(j).wait_send()
    for which in range(2):
        for p in range(2):
            mat_copy(which, 0, p).wait_send()
            mat_copy(which, 1, p).wait_send()
            mat_relay(which, p).wait_send()
            for i in range(GROUP):
                mat_cross(which, i, p).wait_send()
    old_cross().wait_send()
    done_halo(0, 0)
    for n in range(1, ORDER + 1):
        for c in range(CHUNKS):
            done_halo(n, c)

    @pl.loop(1, spaces)
    def _(j):
        part_copy(j).wait_recv()

    sums = []
    for g in range(GROUP):
        value = got[g]
        for r in range(1, quads):
            value = value + got[r * GROUP + g]
        sums.append(value * (1.0 / (spaces * BLOCK)))
    for t in range(2):
        columns = slice(t * LANES, (t + 1) * LANES)
        proj[0, :, columns], proj[1, :, columns] = pair(even, sums[2 * t], sums[2 * t + 1])

    @pl.loop(1, spaces)
    def _(j):
        part_copy(j).wait_send()


def solution(mesh):
    spaces = mesh.shape["space"]
    dma = pltpu.SemaphoreType.DMA
    f32, bf16 = jnp.float32, jnp.bfloat16

    def local(coefficients, margin, step_matrix, neighbours, pattern):
        share = 2 * coefficients.shape[3] // spaces
        vmem = pl.BlockSpec(memory_space=pltpu.VMEM)
        hbm = pl.BlockSpec(memory_space=pltpu.HBM)
        return pl.pallas_call(
            functools.partial(kernel, spaces),
            out_shape=(
                jax.ShapeDtypeStruct(coefficients.shape, f32),
                jax.ShapeDtypeStruct((2, share, coefficients.shape[3]), f32),
            ),
            in_specs=[hbm] * 5,
            out_specs=(vmem, vmem),
            scratch_shapes=[
                pltpu.VMEM((2,) + coefficients.shape[2:], f32),
                pltpu.VMEM((2, margin.shape[1], HALF, BLOCK), f32),
                pltpu.SMEM(neighbours.shape, jnp.int32),
                pltpu.SMEM(pattern.shape, jnp.int32),
                dma((5,)),
                pltpu.VMEM((2, GROUP, GROUP, BLOCK, LANES), f32),
                pltpu.VMEM((2, REACH, BLOCK, LANES), f32),
                pltpu.VMEM((ORDER, CHUNKS, 2, BLOCK, LANES), f32),
                pltpu.VMEM((ORDER, CHUNKS, 2, BLOCK, LANES), f32),
                pltpu.VMEM((2, GROUP, 2, 2, HALF // 2, WIN * BLOCK), f32),
                pltpu.VMEM((2, GROUP, 2 * BLOCK, WIN * BLOCK), bf16),
                pltpu.VMEM((CHUNKS, (2 * REACH + GROUP) * BLOCK, LANES), bf16),
                pltpu.VMEM((CHUNKS, 2, BLOCK, LANES), f32),
                pltpu.VMEM((GROUP, BLOCK, LANES), f32),
                pltpu.VMEM((GROUP * BLOCK, 2 * LANES), bf16),
                pltpu.VMEM((2 * GROUP, LANES, GROUP * BLOCK), bf16),
                pltpu.VMEM((2 * GROUP, LANES, GROUP * BLOCK), bf16),
                pltpu.VMEM((spaces, share, LANES), f32),
                pltpu.VMEM((spaces, share, LANES), f32),
                pltpu.VMEM((GROUP, BLOCK, LANES), f32),
                dma((GROUP,)), dma((GROUP,)),
                dma((2, 2, 2)), dma((2, 2, 2)),
                dma((2, 2)), dma((2, 2)),
                dma((2, GROUP, 2)), dma((2, GROUP, 2)),
                dma((GROUP, GROUP)), dma((GROUP, GROUP)),
                dma, dma,
                dma((ORDER + 1, CHUNKS, 2)), dma((ORDER + 1, CHUNKS, 2)),
                dma((GROUP,)), dma((GROUP,)),
                dma((spaces,)), dma((spaces,)),
            ],
            compiler_params=pltpu.CompilerParams(
                collective_id=0, has_side_effects=True, vmem_limit_bytes=64 * 1024 * 1024
            ),
            cost_estimate=pl.CostEstimate(flops=1200000000, bytes_accessed=3000000, transcendentals=0),
        )(coefficients, margin, step_matrix, neighbours, pattern)

    return jax.shard_map(
        local,
        mesh=mesh,
        in_specs=(
            P(None, "space", None, "orb"),
            P("space", None, None, None),
            P("space", None, None, None),
            P("space", None),
            P("space", None),
        ),
        out_specs=(P(None, "space", None, "orb"), P(None, "space", "orb")),
        check_vma=False,
    )
```

```python
import functools

import jax
import jax.numpy as jnp
from jax import lax
from jax.experimental import pallas as pl
from jax.experimental.pallas import tpu as pltpu
from jax.sharding import PartitionSpec as P

REACH = 2
WIN = 2 * REACH + 1
ORDER = 4
GROUP = 4
BLOCK = 128
LANES = 128
HALF = BLOCK // 2
MESH = pl.DeviceIdType.MESH


CHUNKS = 2
QUARTER = LANES // 4


def lanes():
    return lax.broadcasted_iota(jnp.int32, (1, LANES), 1)


def pair(even, first, second):
    ahead = jnp.where(even, first, pltpu.roll(second, QUARTER, 1))
    behind = jnp.where(even, pltpu.roll(first, LANES - QUARTER, 1), second)
    return ahead, behind


def swap(even, value):
    return jnp.where(even, pltpu.roll(value, LANES - QUARTER, 1), pltpu.roll(value, QUARTER, 1))


def cross(left, first, second):
    ahead = jnp.where(left, first, pltpu.roll(second, LANES // 2, 1))
    behind = jnp.where(left, pltpu.roll(first, LANES // 2, 1), second)
    return ahead, behind


def split(value):
    high = value.astype(jnp.bfloat16)
    low = (value - high.astype(jnp.float32)).astype(jnp.bfloat16)
    return high, low


def product(high, low, both):
    wide = jnp.dot(high, both, preferred_element_type=jnp.float32)
    narrow = jnp.dot(low, both[:, :LANES], preferred_element_type=jnp.float32)
    return wide[:, :LANES] + wide[:, LANES:] + narrow


def kernel(
    spaces, coef_in, margin_in, step_in, nbr_in, pat_in, prop, proj,
    coef, raw, nbr, pat, load_sem, old, edge, halo, state, rows, mat, both, acc, total, blocks_new, new, old_hi, old_lo, part, got, back,
    a2a_s, a2a_r, mat_s, mat_r, dia_s, dia_r, fwd_s, fwd_r, old_s, old_r, oldx_s, oldx_r,
    halo_s, halo_r, back_s, back_r, part_s, part_r,
):
    share = proj.shape[1]
    quads = spaces // GROUP
    s = lax.axis_index("space")
    o = lax.axis_index("orb")
    q = s // GROUP
    m = s % GROUP
    base = q * GROUP
    other = 1 - o
    left = lanes() < LANES // 2
    even = lanes() % (2 * QUARTER) < QUARTER
    beside = (m + 1 - 2 * (m % 2), (m + GROUP // 2) % GROUP)
    blocks = (m, beside[0], beside[1], (beside[0] + GROUP // 2) % GROUP)
    mine = pl.ds(pl.multiple_of(o * HALF, HALF), HALF)

    loads = [
        pltpu.make_async_copy(coef_in.at[:, 0], coef, load_sem.at[0]),
        pltpu.make_async_copy(nbr_in, nbr, load_sem.at[1]),
        pltpu.make_async_copy(pat_in, pat, load_sem.at[2]),
        pltpu.make_async_copy(margin_in.at[0, :, mine], raw.at[0], load_sem.at[3]),
        pltpu.make_async_copy(step_in.at[0, :, mine], raw.at[1], load_sem.at[4]),
    ]
    for load in loads:
        load.start()

    barrier = pltpu.get_barrier_semaphore()

    @pl.loop(1, spaces)
    def _(j):
        pl.semaphore_signal(barrier, inc=1, device_id=((s + j) % spaces, o), device_id_type=MESH)

    pl.semaphore_signal(barrier, inc=1, device_id=(s, other), device_id_type=MESH)

    loads[0].wait()
    for t in range(2):
        columns = slice(t * LANES, (t + 1) * LANES)
        real = coef[0, :, columns]
        imag = coef[1, :, columns]
        old[o, 2 * t, m], old[o, 2 * t + 1, m] = pair(even, real, imag)

    def compact(which):
        scales = []
        for k in range(nbr.shape[1]):
            live = jnp.float32(1.0) if k == 0 else pat[0, k].astype(jnp.float32)
            scales.append([(nbr[0, k] == s + (d - REACH)).astype(jnp.float32) * live for d in range(WIN)])
        deep = HALF // 4

        @pl.loop(0, 4)
        def _(i):
            sums = [None] * WIN
            for k in range(nbr.shape[1]):
                block = raw[which, k, pl.ds(pl.multiple_of(i * deep, deep), deep), :]
                for d in range(WIN):
                    value = scales[k][d] * block
                    sums[d] = value if sums[d] is None else sums[d] + value
            for d in range(WIN):
                at = pl.ds(pl.multiple_of((i % 2) * deep, deep), deep)
                rows[which, m, o, i // 2, at, d * BLOCK:(d + 1) * BLOCK] = sums[d]

    def clear(side):
        zero = jnp.zeros((BLOCK, LANES), jnp.float32)
        for w in range(REACH):
            edge[side, w] = zero
        for n in range(ORDER):
            for c in range(CHUNKS):
                halo[n, c, side] = zero

    @pl.when(q == 0)
    def _():
        clear(0)

    @pl.when(q == quads - 1)
    def _():
        clear(1)

    pl.semaphore_wait(barrier, spaces)

    def remote(src, dst, send, recv, where):
        return pltpu.make_async_remote_copy(
            src_ref=src, dst_ref=dst, send_sem=send, recv_sem=recv, device_id=where, device_id_type=MESH
        )

    def peer(j):
        return (m + j) % GROUP

    def a2a(j):
        return remote(old.at[o, peer(j), m], old.at[o, peer(j), m], a2a_s.at[j], a2a_r.at[j], (base + peer(j), o))

    def mat_copy(which, axis, p):
        src = rows.at[which, m, o, p]
        return remote(src, src, mat_s.at[which, axis, p], mat_r.at[which, axis, p], (base + beside[axis], o))

    def mat_relay(which, p):
        src = rows.at[which, beside[p], o, p]
        return remote(src, src, dia_s.at[which, p], dia_r.at[which, p], (base + beside[1 - p], o))

    def mat_cross(which, i, p):
        src = rows.at[which, blocks[i], o, p]
        return remote(src, src, fwd_s.at[which, i, p], fwd_r.at[which, i, p], (s, other))

    def old_copy(j, i):
        g = (m + j + i) % GROUP
        return remote(old.at[o, g, m], old.at[o, g, m], old_s.at[j, i], old_r.at[j, i], (base + peer(j), o))

    def old_cross():
        return remote(old.at[o], old.at[o], oldx_s, oldx_r, (s, other))

    def halo_copy(n, c, up):
        side = 0 if up else 1
        if isinstance(n, int) and n == 0:
            src = old.at[o, m, REACH:GROUP] if up else old.at[o, m, 0:REACH]
            dst = edge.at[side]
        else:
            src, dst = state.at[n - 1, c, 1 - side], halo.at[n - 1, c, side]
        to = s + GROUP if up else s - GROUP
        return remote(src, dst, halo_s.at[n, c, side], halo_r.at[n, c, side], (to, o))

    def send_halo(n, c):
        @pl.when(q < quads - 1)
        def _():
            halo_copy(n, c, True).start()

        @pl.when(q > 0)
        def _():
            halo_copy(n, c, False).start()

    def wait_halo(n, c):
        @pl.when(q > 0)
        def _():
            halo_copy(n, c, True).wait_recv()

        @pl.when(q < quads - 1)
        def _():
            halo_copy(n, c, False).wait_recv()

    def done_halo(n, c):
        @pl.when(q < quads - 1)
        def _():
            halo_copy(n, c, True).wait_send()

        @pl.when(q > 0)
        def _():
            halo_copy(n, c, False).wait_send()

    def halves(value):
        high = value.astype(jnp.bfloat16).astype(jnp.float32)
        ahead, behind = cross(left, high, value - high)
        return ahead.astype(jnp.bfloat16), behind.astype(jnp.bfloat16)

    def span(w):
        return slice(w * BLOCK, (w + 1) * BLOCK)

    def put_block(w, value):
        both[0, span(w)], both[1, span(w)] = halves(value)

    def put_pair(c, w, value):
        both[c, span(w)], both[c, span(w + 1)] = halves(value)

    for j in range(1, GROUP):
        a2a(j).start()
    for load in loads[1:4]:
        load.wait()

    def send_matrix(which):
        for p in range(2):
            mat_copy(which, p, p).start()
        for p in range(2):
            mat_copy(which, 1 - p, p).start()
        for p in range(2):
            mat_cross(which, 0, p).start()

    def relay_matrix(which):
        for p in range(2):
            mat_copy(which, p, p).wait_recv()
            mat_relay(which, p).start()
            mat_cross(which, 1 + p, p).start()

    compact(0)
    send_matrix(0)
    loads[4].wait()
    compact(1)

    for j in range(1, GROUP):
        a2a(j).wait_recv()
    send_halo(0, 0)
    for b in range(GROUP):
        put_block(REACH + b, old[o, m, b])
    relay_matrix(0)
    send_matrix(1)

    def receive_matrix(which):
        for p in range(2):
            mat_copy(which, 1 - p, p).wait_recv()
            mat_cross(which, 2 - p, p).start()
        for p in range(2):
            mat_relay(which, p).wait_recv()
            mat_cross(which, 3, p).start()
        for i in range(GROUP):
            for p in range(2):
                mat_cross(which, i, p).wait_recv()
        @pl.loop(0, GROUP)
        def _(b):
            for h in range(2):
                high, low = split(rows[which, b, h].reshape(HALF, WIN * BLOCK))
                mat[which, b, h * HALF:(h + 1) * HALF] = high
                mat[which, b, BLOCK + h * HALF:BLOCK + (h + 1) * HALF] = low

    def piece(which, c, b, first, last):
        columns = slice((first - b) * BLOCK, (last - b) * BLOCK)
        value = jnp.dot(
            mat[which, b, :, columns], both[c, first * BLOCK:last * BLOCK], preferred_element_type=jnp.float32
        )
        return value[:BLOCK] + value[BLOCK:]

    def inner(which, c):
        for b in range(GROUP):
            acc[c, b] = piece(which, c, b, max(b, REACH), min(b + WIN, REACH + GROUP))

    def outer(which, c):
        result = []
        for b in range(GROUP):
            value = acc[c, b]
            if b < REACH:
                value = value + piece(which, c, b, b, REACH)
            if b + WIN > REACH + GROUP:
                value = value + piece(which, c, b, REACH + GROUP, b + WIN)
            result.append(value + pltpu.roll(value, LANES // 2, 1))
        return [jnp.where(left, result[2 * i], result[2 * i + 1]) for i in range(GROUP // 2)]

    receive_matrix(0)
    both_chunks = functools.partial(pl.loop, 0, CHUNKS)

    @both_chunks()
    def _(c):
        inner(0, c)

    wait_halo(0, 0)
    for side in range(2):
        for w in range(REACH):
            put_block(side * (REACH + GROUP) + w, edge[side, w])
    for i in range(GROUP // 2):
        state[0, 0, i], state[0, 1, i] = cross(left, old[o, m, 2 * i], old[o, m, 2 * i + 1])

    @both_chunks()
    def _(c):
        image = outer(0, c)
        for i in range(GROUP // 2):
            moved = state[0, c, i] + image[i]
            state[0, c, i] = moved
            total[c, i] = moved
        send_halo(1, c)
        for i in range(GROUP // 2):
            put_pair(c, REACH + 2 * i, total[c, i])

    relay_matrix(1)
    for j in range(1, GROUP):
        for i in range(1, GROUP):
            old_copy(j, i).start()
    receive_matrix(1)

    def turn(core):
        @pl.loop(0, GROUP)
        def _(g):
            high, low = split(old[core, g].reshape(GROUP * BLOCK, LANES).T)
            old_hi[core * GROUP + g] = high
            old_lo[core * GROUP + g] = low

    @both_chunks()
    def _(c):
        inner(1, c)

    @pl.loop(1, ORDER + 1)
    def _(n):
        @pl.when(n == ORDER - 1)
        def _():
            for j in range(1, GROUP):
                for i in range(1, GROUP):
                    old_copy(j, i).wait_recv()
            old_cross().start()

        @pl.when(n == ORDER)
        def _():
            old_cross().wait_recv()

        @pl.when(n >= ORDER - 1)
        def _():
            turn((o + n + ORDER - 1) % 2)

        scale = jnp.where(even, jnp.float32(1.0), jnp.float32(-1.0)) / n.astype(jnp.float32)

        @both_chunks()
        def _(c):
            wait_halo(n, c)
            for side in range(2):
                put_pair(c, side * (REACH + GROUP), halo[n - 1, c, side])
            terms = [swap(even, value) * scale for value in outer(1, c)]
            for i in range(GROUP // 2):
                total[c, i] = total[c, i] + terms[i]

            @pl.when(n < ORDER)
            def _():
                for i in range(GROUP // 2):
                    state[n, c, i] = terms[i]
                send_halo(n + 1, c)
                for i in range(GROUP // 2):
                    put_pair(c, REACH + 2 * i, terms[i])
                inner(1, c)

    for i in range(GROUP // 2):
        ends = cross(left, total[0, i], total[1, i])
        for h in range(2):
            blocks_new[2 * i + h] = ends[h]
            high, low = split(ends[h])
            new[span(2 * i + h), :LANES] = high
            new[span(2 * i + h), LANES:] = low

    def back_copy(j):
        return remote(blocks_new.at[peer(j)], back.at[m], back_s.at[j], back_r.at[j], (base + peer(j), o))

    for j in range(1, GROUP):
        back_copy(j).start()
    back[m] = blocks_new[m]

    sign = jnp.where(even, jnp.float32(1.0), jnp.float32(-1.0))
    per = QUARTER // share

    def part_copy(j):
        to = (s + j) % spaces
        return remote(part.at[to], got.at[s], part_s.at[j], part_r.at[j], (to, o))

    @pl.loop(0, 2 * GROUP)
    def _(i):
        g = (i + (q + quads // 2) * 2 * GROUP // quads) % (2 * GROUP)
        value = product(old_hi[g], old_lo[g], new[...])
        for c in range(CHUNKS):
            lead = 2 * c * QUARTER
            found = value[lead:lead + QUARTER] + swap(even, value[lead + QUARTER:lead + 2 * QUARTER]) * sign
            first = ((g // 2) * 4 + 2 * c + g % 2) * per
            for r in range(per):
                to = first + r
                part[to] = found[r * share:(r + 1) * share]

                @pl.when(to != s)
                def _():
                    part_copy((to - s + spaces) % spaces).start()

    got[s] = part[s]

    for j in range(1, GROUP):
        back_copy(j).wait_recv()
    for t in range(2):
        columns = slice(t * LANES, (t + 1) * LANES)
        prop[0, 0, :, columns], prop[1, 0, :, columns] = pair(even, back[2 * t], back[2 * t + 1])

    for j in range(1, GROUP):
        a2a(j).wait_send()
        for i in range(1, GROUP):
            old_copy(j, i).wait_send()
        back_copy(j).wait_send()
    for which in range(2):
        for p in range(2):
            mat_copy(which, 0, p).wait_send()
            mat_copy(which, 1, p).wait_send()
            mat_relay(which, p).wait_send()
            for i in range(GROUP):
                mat_cross(which, i, p).wait_send()
    old_cross().wait_send()
    done_halo(0, 0)
    for n in range(1, ORDER + 1):
        for c in range(CHUNKS):
            done_halo(n, c)

    @pl.loop(1, spaces)
    def _(j):
        part_copy(j).wait_recv()

    sums = []
    for g in range(GROUP):
        value = got[g]
        for r in range(1, quads):
            value = value + got[r * GROUP + g]
        sums.append(value * (1.0 / (spaces * BLOCK)))
    for t in range(2):
        columns = slice(t * LANES, (t + 1) * LANES)
        proj[0, :, columns], proj[1, :, columns] = pair(even, sums[2 * t], sums[2 * t + 1])

    @pl.loop(1, spaces)
    def _(j):
        part_copy(j).wait_send()


def solution(mesh):
    spaces = mesh.shape["space"]
    dma = pltpu.SemaphoreType.DMA
    f32, bf16 = jnp.float32, jnp.bfloat16

    def local(coefficients, margin, step_matrix, neighbours, pattern):
        share = 2 * coefficients.shape[3] // spaces
        vmem = pl.BlockSpec(memory_space=pltpu.VMEM)
        hbm = pl.BlockSpec(memory_space=pltpu.HBM)
        return pl.pallas_call(
            functools.partial(kernel, spaces),
            out_shape=(
                jax.ShapeDtypeStruct(coefficients.shape, f32),
                jax.ShapeDtypeStruct((2, share, coefficients.shape[3]), f32),
            ),
            in_specs=[hbm] * 5,
            out_specs=(vmem, vmem),
            scratch_shapes=[
                pltpu.VMEM((2,) + coefficients.shape[2:], f32),
                pltpu.VMEM((2, margin.shape[1], HALF, BLOCK), f32),
                pltpu.SMEM(neighbours.shape, jnp.int32),
                pltpu.SMEM(pattern.shape, jnp.int32),
                dma((5,)),
                pltpu.VMEM((2, GROUP, GROUP, BLOCK, LANES), f32),
                pltpu.VMEM((2, REACH, BLOCK, LANES), f32),
                pltpu.VMEM((ORDER, CHUNKS, 2, BLOCK, LANES), f32),
                pltpu.VMEM((ORDER, CHUNKS, 2, BLOCK, LANES), f32),
                pltpu.VMEM((2, GROUP, 2, 2, HALF // 2, WIN * BLOCK), f32),
                pltpu.VMEM((2, GROUP, 2 * BLOCK, WIN * BLOCK), bf16),
                pltpu.VMEM((CHUNKS, (2 * REACH + GROUP) * BLOCK, LANES), bf16),
                pltpu.VMEM((CHUNKS, GROUP, BLOCK, LANES), f32),
                pltpu.VMEM((CHUNKS, 2, BLOCK, LANES), f32),
                pltpu.VMEM((GROUP, BLOCK, LANES), f32),
                pltpu.VMEM((GROUP * BLOCK, 2 * LANES), bf16),
                pltpu.VMEM((2 * GROUP, LANES, GROUP * BLOCK), bf16),
                pltpu.VMEM((2 * GROUP, LANES, GROUP * BLOCK), bf16),
                pltpu.VMEM((spaces, share, LANES), f32),
                pltpu.VMEM((spaces, share, LANES), f32),
                pltpu.VMEM((GROUP, BLOCK, LANES), f32),
                dma((GROUP,)), dma((GROUP,)),
                dma((2, 2, 2)), dma((2, 2, 2)),
                dma((2, 2)), dma((2, 2)),
                dma((2, GROUP, 2)), dma((2, GROUP, 2)),
                dma((GROUP, GROUP)), dma((GROUP, GROUP)),
                dma, dma,
                dma((ORDER + 1, CHUNKS, 2)), dma((ORDER + 1, CHUNKS, 2)),
                dma((GROUP,)), dma((GROUP,)),
                dma((spaces,)), dma((spaces,)),
            ],
            compiler_params=pltpu.CompilerParams(
                collective_id=0, has_side_effects=True, vmem_limit_bytes=64 * 1024 * 1024
            ),
            cost_estimate=pl.CostEstimate(flops=1200000000, bytes_accessed=3000000, transcendentals=0),
        )(coefficients, margin, step_matrix, neighbours, pattern)

    return jax.shard_map(
        local,
        mesh=mesh,
        in_specs=(
            P(None, "space", None, "orb"),
            P("space", None, None, None),
            P("space", None, None, None),
            P("space", None),
            P("space", None),
        ),
        out_specs=(P(None, "space", None, "orb"), P(None, "space", "orb")),
        check_vma=False,
    )
```
